32 devices in a mesh: space: 8 (over y, x, core), band: 4 (over z).
Axes of the slice: x: 2, y: 2, z: 4, core: 2. Of those that a mesh axis runs over, the one named last changes fastest.
Arguments:
- vectors: float32 [32768, 1024], P('space', 'band')
- blocks: float32 [128, 7, 256, 256], P('space'), may hold values from -0.125 to 0.125
- neighbours: int32 [128, 7], P('space'), may hold values from 0 to 127, as said below
Outputs:
- rotated: float32 [32768, 1024], P('space', 'band')
The draws below stay inside these ranges and needn't reach their ends.
Inputs may be any that keep to these rules, and one draw needn't show every extreme that they name: neighbours[e, k] lies within 2 places of e in the cyclic order of the elements; for every e, neighbours[e, 1] = e - 2 and neighbours[e, 2] = e + 2, taken modulo 128.
All inputs are finite; a program needn't handle non-finite values.
Results may differ from the reference program's by a relative error of at most 0.000098.
Values sent between devices are 32-bit elements; how exact they have to be, the bound alone decides.
A program may use at most 128 MiB of HBM per device.

```python
import math
import jax
import jax.numpy as jnp
from jax import lax

BASIS = 256
VECTORS = 1024
REACH = 2
ELEMENTS = 128
ORDER = 32768


def draw_neighbours(key, part):
    element_ids = jnp.arange(ELEMENTS, dtype=jnp.int32)[:, None]
    offsets = jax.random.randint(jax.random.fold_in(key, 11), (ELEMENTS, 7), -REACH, REACH + 1, dtype=jnp.int32)
    offsets = offsets.at[:, 1].set(-REACH).at[:, 2].set(REACH)
    return ((element_ids + offsets + ELEMENTS) % ELEMENTS).astype(jnp.int32)


def draw_vectors(key, part):
    key_base = jax.random.fold_in(key, 21)
    key_rows = jax.random.fold_in(key, 22)
    key_cols = jax.random.fold_in(key, 23)
    row_index = jnp.arange(ORDER, dtype=jnp.float32)[:, None]
    rising = jnp.exp(math.log(3.0) * row_index / ORDER)
    row_scale = jnp.exp(jax.random.uniform(key_rows, (ORDER, 1), jnp.float32, 0.0, math.log(10.0))) * rising
    base = jnp.clip(jax.random.normal(key_base, (ORDER, VECTORS), jnp.float32), -6.0, 6.0)
    col_scale = jnp.exp(jax.random.uniform(key_cols, (1, VECTORS), jnp.float32, 0.0, math.log(10.0)))
    return base * row_scale * col_scale


def levels(stream_key, dims, cuts, low, largest):
    level, own = 1.0, jax.random.fold_in(stream_key, 6)
    for axis_at, parts in cuts:
        heights = jnp.exp(jax.random.uniform(jax.random.fold_in(own, axis_at), (parts,), jnp.float32, low / len(cuts), largest / len(cuts)))
        level = level * jnp.repeat(heights, dims[axis_at] // parts).reshape([-1 if axis == axis_at else 1 for axis in range(len(dims))])
    return level


def bell_draw(stream_key, extent, spread, reach, split=(), kind=jnp.bfloat16):
    factor_of = levels(stream_key, extent, split, -0.22, 0.18) if split else 1.0
    values = jax.random.normal(stream_key, extent, jnp.float32) * spread * factor_of
    return jnp.minimum(jnp.maximum(values, -reach), reach).astype(kind)


def setup_inputs(seed: int = 0) -> dict:
    seeds = jax.random.split(jax.random.key(seed), 4)
    return {
        "vectors": draw_vectors(jax.random.fold_in(seeds[3], 71), 0),
        "blocks": bell_draw(seeds[1], (ELEMENTS, 7, BASIS, BASIS), (7 * BASIS) ** -0.5, 0.125, ((0, 8),), jnp.float32),
        "neighbours": draw_neighbours(jax.random.fold_in(seeds[3], 71), 0),
    }


def apply_operator(field, blocks, neighbours):
    elements = field.reshape(ELEMENTS, BASIS, VECTORS)

    def element_term(pair):
        element_blocks, element_ids = pair
        picked = elements[element_ids]
        return jnp.einsum('kij,kjm->im', element_blocks, picked, precision=lax.Precision.HIGHEST)
    result = lax.map(element_term, (blocks, neighbours))
    return result.reshape(ORDER, VECTORS)

def reference(vectors, blocks, neighbours):
    first_step = (apply_operator(vectors, blocks, neighbours) - 0.5 * vectors) / 1.5
    filtered = 2.0 * (apply_operator(first_step, blocks, neighbours) - 0.5 * first_step) / 1.5 - vectors
    gram = jnp.dot(filtered.T, filtered, precision=lax.Precision.HIGHEST, preferred_element_type=jnp.float32)
    scale = jnp.trace(gram) / VECTORS
    normed = gram / scale
    identity = jnp.eye(VECTORS, dtype=jnp.float32)
    squared = jnp.dot(normed, normed, precision=lax.Precision.HIGHEST, preferred_element_type=jnp.float32)
    poly = (15.0 * identity - 10.0 * normed + 3.0 * squared) / 8.0
    result = jnp.dot(filtered, poly, precision=lax.Precision.HIGHEST, preferred_element_type=jnp.float32)
    return result * jnp.sqrt(ORDER / scale)
```

```python
import functools

import jax
import jax.numpy as jnp
from jax import lax
from jax.experimental import pallas as pl
from jax.experimental.pallas import tpu as pltpu
from jax.sharding import PartitionSpec as P

REACH = 2
SPAN = 2 * REACH + 1
LANES = 128
MESH = pl.DeviceIdType.MESH
F32 = jnp.float32
BF16 = jnp.bfloat16


def split(x):
    high = x.astype(BF16)
    return high, (x - high.astype(F32)).astype(BF16)


def dot3(a, b):
    (ah, al), (bh, bl) = a, b
    mul = functools.partial(jnp.dot, preferred_element_type=F32)
    return mul(ah, bh) + (mul(ah, bl) + mul(al, bh))


def combine_kernel(slots, blocks, high, low, total):
    e = pl.program_id(0)
    basis = blocks.shape[2]
    total[0] = blocks[0, 1]
    total[SPAN - 1] = blocks[0, 2]
    for o in range(1, SPAN - 1):
        total[o] = jnp.zeros((basis, basis), F32)
    for k in range(blocks.shape[1]):
        if k not in (1, 2):
            slot = slots[e, k]
            total[slot] += blocks[0, k]
    for o in range(SPAN):
        high[0, :, o * basis:(o + 1) * basis], low[0, :, o * basis:(o + 1) * basis] = split(total[o])


def combine(slots, blocks):
    elem, count, basis, _ = blocks.shape
    out = jax.ShapeDtypeStruct((elem, basis, SPAN * basis), BF16)
    spec = pl.BlockSpec((1, basis, SPAN * basis), lambda e, s: (e, 0, 0))
    return pl.pallas_call(
        combine_kernel,
        grid_spec=pltpu.PrefetchScalarGridSpec(
            num_scalar_prefetch=1,
            grid=(elem,),
            in_specs=[pl.BlockSpec((1, count, basis, basis), lambda e, s: (e, 0, 0, 0))],
            out_specs=[spec, spec],
            scratch_shapes=[pltpu.VMEM((SPAN, basis, basis), F32)],
        ),
        out_shape=[out, out],
        compiler_params=pltpu.CompilerParams(vmem_limit_bytes=32 * 2**20),
        name="combine",
    )(slots, blocks)


def main_kernel(
    n_s, n_b, elem, basis, panel, parts,
    v_hbm, wh_hbm, wl_hbm, out,
    x, xh, xl, fh, fl, wh, wl, f1, recv, g, ar, whole, halo,
    load_sem, w_sem, halo_send, halo_recv, a2a_send, a2a_recv, ar_send, ar_recv,
    back_send, back_recv, own_sem,
):
    s, b = lax.axis_index("space"), lax.axis_index("band")
    per_home = elem // n_b
    home_rows = per_home * basis
    edge = REACH * basis
    vectors = n_b * panel
    order = n_s * elem * basis
    up, down = lax.rem(s + 1, n_s), lax.rem(s + n_s - 1, n_s)

    def rows_of(e):
        return pl.ds(pl.multiple_of(e * basis, basis), basis)

    def band_at(d):
        return lax.rem(b + d, n_b)

    def xor(index, bit):
        return index + bit * (1 - 2 * lax.rem(index // bit, 2))

    space_bits = [1 << k for k in range(n_s.bit_length() - 1)]
    band_bits = [1 << k for k in range(n_b.bit_length() - 1)]

    loads = [pltpu.make_async_copy(v_hbm, x, load_sem)]
    loads[0].start()

    def w_copies(e):
        return (
            pltpu.make_async_copy(wh_hbm.at[e], wh.at[e], w_sem.at[0, e]),
            pltpu.make_async_copy(wl_hbm.at[e], wl.at[e], w_sem.at[1, e]),
        )

    def start_w(e, carry):
        for copy in w_copies(e):
            copy.start()
        return carry

    lax.fori_loop(0, elem, start_w, 0)

    barrier = pltpu.get_barrier_semaphore()
    peers = [(up, b), (down, b)]
    peers += [(s, band_at(d)) for d in range(1, n_b)]
    peers += [(xor(s, bit), b) for bit in space_bits]
    for peer in peers:
        pl.semaphore_signal(barrier, inc=1, device_id=peer, device_id_type=MESH)
    pl.semaphore_wait(barrier, len(peers))

    def halo_copies(step, field):
        def copy(src, side, target):
            return pltpu.make_async_remote_copy(
                src_ref=src, dst_ref=halo.at[step, side],
                send_sem=halo_send.at[step, side], recv_sem=halo_recv.at[step, side],
                device_id=(target, b), device_id_type=MESH)
        last = field.at[pl.ds(elem * basis - edge, edge)]
        first = field.at[pl.ds(0, edge)]
        return copy(last, 0, up), copy(first, 1, down)

    def take_halo(step, copies, high, low):
        for side, copy in enumerate(copies):
            copy.wait_recv()
            start = side * (elem + REACH) * basis
            high[pl.ds(start, edge)], low[pl.ds(start, edge)] = split(halo[step, side])

    def applied(e, high, low):
        near = pl.ds(pl.multiple_of(e * basis, basis), SPAN * basis)
        return dot3((wh[e], wl[e]), (high[near], low[near]))

    loads[0].wait()
    halo1 = halo_copies(0, x)
    for copy in halo1:
        copy.start()

    def split_x(e, carry):
        at = rows_of(e + REACH)
        xh[at], xl[at] = split(x[rows_of(e)])
        return carry

    lax.fori_loop(0, elem, split_x, 0)

    def first_apply(e, carry):
        for copy in w_copies(e):
            copy.wait()
        value = (applied(e, xh, xl) - 0.5 * x[rows_of(e)]) / 1.5
        f1[rows_of(e)] = value
        at = rows_of(e + REACH)
        fh[at], fl[at] = split(value)
        return carry

    ahead = REACH + (elem - 2 * REACH) // 3
    lax.fori_loop(REACH, ahead, first_apply, 0)
    take_halo(0, halo1, xh, xl)
    lax.fori_loop(0, REACH, first_apply, 0)
    lax.fori_loop(elem - REACH, elem, first_apply, 0)
    halo2 = halo_copies(1, f1)
    for copy in halo2:
        copy.start()
    lax.fori_loop(ahead, elem - REACH, first_apply, 0)
    for copy in halo1:
        copy.wait_send()
    take_halo(1, halo2, fh, fl)

    def filtered_of(e):
        mine = rows_of(e)
        return 2.0 * (applied(e, fh, fl) - 0.5 * f1[mine]) / 1.5 - x[mine]

    def to_home(c, d):
        home = band_at(d)
        return pltpu.make_async_remote_copy(
            src_ref=x.at[rows_of(home * per_home + c)],
            dst_ref=recv.at[rows_of(b * per_home + c)],
            send_sem=a2a_send.at[c, d], recv_sem=a2a_recv.at[c, b],
            device_id=(s, home), device_id_type=MESH)

    far_first = sorted(range(1, n_b), key=lambda d: -min(d, n_b - d))

    def second_apply(c, carry):
        for d in far_first:
            e = band_at(d) * per_home + c
            x[rows_of(e)] = filtered_of(e)
            to_home(c, d).start()
        e = b * per_home + c
        recv[rows_of(e)] = filtered_of(e)
        return carry

    lax.fori_loop(0, per_home, second_apply, 0)
    for copy in halo2:
        copy.wait_send()

    pairs = [(i, j) for i in range(n_b) for j in range(i, n_b)]
    cuts = panel // LANES
    g[...] = jnp.zeros_like(g)

    def from_home(c, d):
        source = band_at(d)
        return pltpu.make_async_remote_copy(
            src_ref=x.at[rows_of(c)],
            dst_ref=recv.at[rows_of(source * per_home + c)],
            send_sem=a2a_send.at[c, d], recv_sem=a2a_recv.at[c, source],
            device_id=(s, source), device_id_type=MESH)

    def add_gram(c, carry):
        for d in range(1, n_b):
            from_home(c, d).wait_recv()
        parts_of = []
        for i in range(n_b):
            at = rows_of(i * per_home + c)
            high, low = split(recv[at])
            xh[at], xl[at] = high, low
            parts_of.append((high, low))
        for i in range(n_b):
            turned = split(recv[rows_of(i * per_home + c)].T)
            for j in range(i, n_b):
                product = dot3(turned, parts_of[j])
                t = pairs.index((i, j))
                for cut in range(cuts):
                    g[pl.ds((t * cuts + cut) * panel, panel)] += product[:, cut * LANES:(cut + 1) * LANES]
        return carry

    lax.fori_loop(0, per_home, add_gram, 0)

    length = g.shape[0] // parts
    orders = []
    for part in range(parts):
        low_bits, high_bits = [("s", bit) for bit in space_bits], [("b", bit) for bit in band_bits]
        if part % 2:
            low_bits, high_bits = low_bits[:1] + low_bits[1:][::-1], high_bits[::-1]
        orders.append(low_bits + high_bits)
    steps = len(orders[0])

    def partner(kind, bit):
        if kind == "s":
            return (xor(s, bit), b), lax.rem(s // bit, 2)
        return (s, xor(b, bit)), lax.rem(b // bit, 2)

    starts = [part * length for part in range(parts)]
    trail = []
    offset = 0
    for k in range(steps):
        half = length >> (k + 1)
        copies, keeps = [], []
        for part in range(parts):
            target, bit = partner(*orders[part][k])
            keep = pl.multiple_of(starts[part] + bit * half, 8)
            give = pl.multiple_of(starts[part] + (1 - bit) * half, 8)
            copy = pltpu.make_async_remote_copy(
                src_ref=g.at[pl.ds(give, half)], dst_ref=ar.at[part, pl.ds(offset, half)],
                send_sem=ar_send.at[0, k, part], recv_sem=ar_recv.at[0, k, part],
                device_id=target, device_id_type=MESH)
            copy.start()
            copies.append(copy)
            keeps.append((keep, give))
        for part in range(parts):
            copies[part].wait()
            g[pl.ds(keeps[part][0], half)] += ar[part, pl.ds(offset, half)]
            starts[part] = keeps[part][0]
        trail.append(keeps)
        offset += half
    for part in range(parts):
        own = pl.ds(starts[part], length >> steps)
        whole[own] = g[own]
    for k in reversed(range(steps)):
        half = length >> (k + 1)
        copies = []
        for part in range(parts):
            target, _ = partner(*orders[part][k])
            keep, give = trail[k][part]
            copy = pltpu.make_async_remote_copy(
                src_ref=whole.at[pl.ds(keep, half)], dst_ref=whole.at[pl.ds(keep, half)],
                send_sem=ar_send.at[1, k, part], recv_sem=ar_recv.at[1, k, part],
                device_id=target, device_id_type=MESH)
            copy.start()
            copies.append(copy)
        for copy in copies:
            copy.wait()

    def gram_block(t):
        return jnp.concatenate(
            [whole[pl.ds((t * cuts + cut) * panel, panel)] for cut in range(cuts)], axis=1)

    eye = (lax.broadcasted_iota(jnp.int32, (panel, panel), 0)
           == lax.broadcasted_iota(jnp.int32, (panel, panel), 1))
    trace = sum(
        jnp.sum(jnp.where(eye, gram_block(pairs.index((i, i))), 0.0), keepdims=True)
        for i in range(n_b))
    scale = trace / vectors
    slabs = vectors // basis

    def put(first, row, column, value):
        slab, at = row // basis, row % basis
        high, low = split(value)
        wh[first + slab, at:at + panel, column:column + panel] = high
        wl[first + slab, at:at + panel, column:column + panel] = low

    for t, (i, j) in enumerate(pairs):
        normed = gram_block(t) / scale
        put(0, i * panel, j * panel, normed)
        if i != j:
            put(0, j * panel, i * panel, normed.T)

    def matrix(first):
        return tuple(
            ref[first:first + slabs, :, :vectors].reshape(vectors, vectors) for ref in (wh, wl))

    def polynomial(r, carry):
        high, low = wh[r, :, :vectors], wl[r, :, :vectors]
        squared = dot3((high, low), matrix(0))
        normed = high.astype(F32) + low.astype(F32)
        shape = (basis, vectors)
        row = lax.broadcasted_iota(jnp.int32, shape, 0) + r * basis
        diagonal = jnp.where(row == lax.broadcasted_iota(jnp.int32, shape, 1), 15.0, 0.0)
        value = split((diagonal - 10.0 * normed + 3.0 * squared) / 8.0)
        wh[slabs + r, :, :vectors], wl[slabs + r, :, :vectors] = value
        return carry

    lax.fori_loop(0, slabs, polynomial, 0)
    gain = jnp.sqrt(order / scale)

    def back(c, d):
        owner = band_at(d)
        return pltpu.make_async_remote_copy(
            src_ref=f1.at[rows_of(owner * per_home + c)],
            dst_ref=out.at[rows_of(b * per_home + c)],
            send_sem=back_send.at[c, d], recv_sem=back_recv.at[c, b],
            device_id=(s, owner), device_id_type=MESH)

    def own_back(c):
        at = rows_of(b * per_home + c)
        return pltpu.make_async_copy(f1.at[at], out.at[at], own_sem.at[c])

    def rotate(c, carry):
        left = tuple(
            jnp.concatenate([ref[rows_of(i * per_home + c)] for i in range(n_b)], axis=1)
            for ref in (xh, xl))
        turned = dot3(left, matrix(slabs)) * gain
        for i in range(n_b):
            f1[rows_of(i * per_home + c)] = turned[:, i * panel:(i + 1) * panel]
        for d in far_first:
            back(c, d).start()
        own_back(c).start()
        return carry

    lax.fori_loop(0, per_home, rotate, 0)

    def finish(c, carry):
        for d in range(1, n_b):
            to_home(c, d).wait_send()
            back(c, d).wait_send()
            source = band_at(d)
            pltpu.make_async_remote_copy(
                src_ref=f1.at[rows_of(c)],
                dst_ref=out.at[rows_of(source * per_home + c)],
                send_sem=back_send.at[c, d], recv_sem=back_recv.at[c, source],
                device_id=(s, source), device_id_type=MESH).wait_recv()
        own_back(c).wait()
        return carry

    lax.fori_loop(0, per_home, finish, 0)


def per_device(n_s, n_b, vectors, blocks, neighbours):
    elem, _, basis, _ = blocks.shape
    panel = vectors.shape[1]
    total = elem * n_s
    ids = lax.axis_index("space") * elem + jnp.arange(elem, dtype=jnp.int32)
    slots = (neighbours - ids[:, None] + REACH + total) % total
    high, low = combine(slots, blocks)

    rows = elem * basis
    per_home = elem // n_b
    devices = n_s * n_b
    need = n_b * (n_b + 1) // 2 * (panel // LANES) * panel
    parts = 2 if need % (16 * devices) == 0 else 1
    unit = 8 * devices * parts
    packed = -(-need // unit) * unit
    steps = devices.bit_length() - 1
    padded = (elem + 2 * REACH) * basis
    dma = pltpu.SemaphoreType.DMA
    any_spec = pl.BlockSpec(memory_space=pl.ANY)
    flops = 2 * rows * panel * 3 * (2 * SPAN * basis) + 6 * rows * panel * 1024 * 3
    return pl.pallas_call(
        functools.partial(main_kernel, n_s, n_b, elem, basis, panel, parts),
        out_shape=jax.ShapeDtypeStruct((rows, panel), F32),
        in_specs=[any_spec] * 3,
        out_specs=any_spec,
        scratch_shapes=[
            pltpu.VMEM((rows, panel), F32),
            pltpu.VMEM((padded, panel), BF16),
            pltpu.VMEM((padded, panel), BF16),
            pltpu.VMEM((padded, panel), BF16),
            pltpu.VMEM((padded, panel), BF16),
            pltpu.VMEM((elem, basis, SPAN * basis), BF16),
            pltpu.VMEM((elem, basis, SPAN * basis), BF16),
            pltpu.VMEM((rows, panel), F32),
            pltpu.VMEM((rows, panel), F32),
            pltpu.VMEM((packed, LANES), F32),
            pltpu.VMEM((parts, packed // parts, LANES), F32),
            pltpu.VMEM((packed, LANES), F32),
            pltpu.VMEM((2, 2, REACH * basis, panel), F32),
            dma, dma((2, elem)), dma((2, 2)), dma((2, 2)),
            dma((per_home, n_b)), dma((per_home, n_b)),
            dma((2, steps, parts)), dma((2, steps, parts)),
            dma((per_home, n_b)), dma((per_home, n_b)), dma((per_home,)),
        ],
        compiler_params=pltpu.CompilerParams(
            collective_id=0, has_side_effects=True, vmem_limit_bytes=60 * 2**20),
        cost_estimate=pl.CostEstimate(
            flops=flops, bytes_accessed=40 * 2**20, transcendentals=0),
        name="filter_and_rotate",
    )(vectors, high, low)


def solution(mesh):
    return jax.shard_map(
        functools.partial(per_device, mesh.shape["space"], mesh.shape["band"]),
        mesh=mesh,
        in_specs=(P("space", "band"), P("space", None, None, None), P("space", None)),
        out_specs=P("space", "band"),
        check_vma=False,
    )
```

```python
import functools

import jax
import jax.numpy as jnp
from jax import lax
from jax.experimental import pallas as pl
from jax.experimental.pallas import tpu as pltpu
from jax.sharding import PartitionSpec as P

REACH = 2
SPAN = 2 * REACH + 1
LANES = 128
MESH = pl.DeviceIdType.MESH
F32 = jnp.float32
BF16 = jnp.bfloat16


def split(x):
    high = x.astype(BF16)
    return high, (x - high.astype(F32)).astype(BF16)


def dot3(a, b):
    (ah, al), (bh, bl) = a, b
    mul = functools.partial(jnp.dot, preferred_element_type=F32)
    return mul(ah, bh) + (mul(ah, bl) + mul(al, bh))


def main_kernel(
    n_s, n_b, elem, basis, panel, parts,
    weights, v_hbm, blocks, out,
    x, xh, xl, fh, fl, wh, wl, f1, recv, g, ar, whole, halo, raw,
    load_sem, raw_sem, halo_send, halo_recv, a2a_send, a2a_recv, ar_send, ar_recv,
    z_send, z_recv,
    back_send, back_recv, own_sem,
):
    s, b = lax.axis_index("space"), lax.axis_index("band")
    per_home = elem // n_b
    home_rows = per_home * basis
    edge = REACH * basis
    vectors = n_b * panel
    order = n_s * elem * basis
    up, down = lax.rem(s + 1, n_s), lax.rem(s + n_s - 1, n_s)

    def rows_of(e):
        return pl.ds(pl.multiple_of(e * basis, basis), basis)

    def band_at(d):
        return lax.rem(b + d, n_b)

    def xor(index, bit):
        return index + bit * (1 - 2 * lax.rem(index // bit, 2))

    space_bits = [1 << k for k in range(n_s.bit_length() - 1)]
    loads = [pltpu.make_async_copy(v_hbm, x, load_sem)]
    loads[0].start()

    count, slots = blocks.shape[1], raw.shape[0]

    def element_at(p):
        return lax.rem(p + elem // 2, elem)

    def raw_copy(p):
        slot = lax.rem(p, slots)
        return pltpu.make_async_copy(blocks.at[element_at(p)], raw.at[slot], raw_sem.at[slot])

    for p in range(slots - 1):
        raw_copy(jnp.int32(p)).start()

    barrier = pltpu.get_barrier_semaphore()
    peers = [(up, b), (down, b)]
    peers += [(s, band_at(d)) for d in range(1, n_b)]
    peers += [(xor(s, bit), b) for bit in space_bits]
    for peer in peers:
        pl.semaphore_signal(barrier, inc=1, device_id=peer, device_id_type=MESH)
    pl.semaphore_wait(barrier, len(peers))

    def halo_copies(step, field):
        def copy(src, side, target):
            return pltpu.make_async_remote_copy(
                src_ref=src, dst_ref=halo.at[step, side],
                send_sem=halo_send.at[step, side], recv_sem=halo_recv.at[step, side],
                device_id=(target, b), device_id_type=MESH)
        last = field.at[pl.ds(elem * basis - edge, edge)]
        first = field.at[pl.ds(0, edge)]
        return copy(last, 0, up), copy(first, 1, down)

    def take_halo(step, copies, high, low):
        for side, copy in enumerate(copies):
            copy.wait_recv()
            start = side * (elem + REACH) * basis
            high[pl.ds(start, edge)], low[pl.ds(start, edge)] = split(halo[step, side])

    def applied(e, high, low):
        near = pl.ds(pl.multiple_of(e * basis, basis), SPAN * basis)
        return dot3((wh[e], wl[e]), (high[near], low[near]))

    loads[0].wait()
    halo1 = halo_copies(0, x)
    for copy in halo1:
        copy.start()

    def split_x(e, carry):
        at = rows_of(e + REACH)
        xh[at], xl[at] = split(x[rows_of(e)])
        return carry

    lax.fori_loop(0, elem, split_x, 0)

    tile = 32

    def merge(p, e):
        raw_copy(p).wait()

        @pl.when(p + slots - 1 < elem)
        def _():
            raw_copy(p + slots - 1).start()

        slot = lax.rem(p, slots)
        weight = [
            [weights[(e * count + k) * SPAN + o] for o in range(SPAN)] for k in range(count)]

        def merge_rows(r, carry):
            at = pl.ds(pl.multiple_of(r * tile, tile), tile)
            blocks_at = [raw[slot, k, at, :] for k in range(count)]
            for o in range(SPAN):
                total = {0: blocks_at[1], SPAN - 1: blocks_at[2]}.get(o)
                for k in range(count):
                    if k not in (1, 2):
                        term = blocks_at[k] * weight[k][o]
                        total = term if total is None else total + term
                columns = slice(o * basis, (o + 1) * basis)
                wh[e, at, columns], wl[e, at, columns] = split(total)
            return carry

        lax.fori_loop(0, basis // tile, merge_rows, 0)

    def first_apply(p, carry):
        e = element_at(p)
        merge(p, e)
        value = (applied(e, xh, xl) - 0.5 * x[rows_of(e)]) / 1.5
        f1[rows_of(e)] = value
        at = rows_of(e + REACH)
        fh[at], fl[at] = split(value)
        return carry

    lax.fori_loop(0, elem // 2 - REACH, first_apply, 0)
    take_halo(0, halo1, xh, xl)
    lax.fori_loop(elem // 2 - REACH, elem // 2 + REACH, first_apply, 0)
    halo2 = halo_copies(1, f1)
    for copy in halo2:
        copy.start()
    lax.fori_loop(elem // 2 + REACH, elem, first_apply, 0)
    for copy in halo1:
        copy.wait_send()
    take_halo(1, halo2, fh, fl)

    def filtered_of(e):
        mine = rows_of(e)
        return 2.0 * (applied(e, fh, fl) - 0.5 * f1[mine]) / 1.5 - x[mine]

    def to_home(c, d):
        home = band_at(d)
        return pltpu.make_async_remote_copy(
            src_ref=x.at[rows_of(home * per_home + c)],
            dst_ref=recv.at[rows_of(b * per_home + c)],
            send_sem=a2a_send.at[c, d], recv_sem=a2a_recv.at[c, b],
            device_id=(s, home), device_id_type=MESH)

    far_first = sorted(range(1, n_b), key=lambda d: -min(d, n_b - d))

    def second_apply(c, carry):
        for d in far_first:
            e = band_at(d) * per_home + c
            x[rows_of(e)] = filtered_of(e)
            to_home(c, d).start()
        e = b * per_home + c
        recv[rows_of(e)] = filtered_of(e)
        return carry

    lax.fori_loop(0, per_home, second_apply, 0)
    for copy in halo2:
        copy.wait_send()

    pairs = [(i, j) for i in range(n_b) for j in range(i, n_b)]
    cuts = panel // LANES
    g[...] = jnp.zeros_like(g)

    def from_home(c, d):
        source = band_at(d)
        return pltpu.make_async_remote_copy(
            src_ref=x.at[rows_of(c)],
            dst_ref=recv.at[rows_of(source * per_home + c)],
            send_sem=a2a_send.at[c, d], recv_sem=a2a_recv.at[c, source],
            device_id=(s, source), device_id_type=MESH)

    def add_gram(c, carry):
        for d in range(1, n_b):
            from_home(c, d).wait_recv()
        parts_of = []
        for i in range(n_b):
            at = rows_of(i * per_home + c)
            high, low = split(recv[at])
            xh[at], xl[at] = high, low
            parts_of.append((high, low))
        for i in range(n_b):
            turned = split(recv[rows_of(i * per_home + c)].T)
            for j in range(i, n_b):
                product = dot3(turned, parts_of[j])
                t = pairs.index((i, j))
                for cut in range(cuts):
                    g[pl.ds((t * cuts + cut) * panel, panel)] += product[:, cut * LANES:(cut + 1) * LANES]
        return carry

    lax.fori_loop(0, per_home, add_gram, 0)

    length = g.shape[0] // parts
    orders = [
        space_bits[:1] + (space_bits[1:][::-1] if part % 2 else space_bits[1:])
        for part in range(parts)]
    steps = len(space_bits)

    def partner(bit):
        return (xor(s, bit), b), lax.rem(s // bit, 2)

    starts = [part * length for part in range(parts)]
    trail = []
    offset = 0
    for k in range(steps):
        half = length >> (k + 1)
        copies, keeps = [], []
        for part in range(parts):
            target, bit = partner(orders[part][k])
            keep = pl.multiple_of(starts[part] + bit * half, 8)
            give = pl.multiple_of(starts[part] + (1 - bit) * half, 8)
            copy = pltpu.make_async_remote_copy(
                src_ref=g.at[pl.ds(give, half)], dst_ref=ar.at[part, pl.ds(offset, half)],
                send_sem=ar_send.at[0, k, part], recv_sem=ar_recv.at[0, k, part],
                device_id=target, device_id_type=MESH)
            copy.start()
            copies.append(copy)
            keeps.append(keep)
        for part in range(parts):
            copies[part].wait()
            g[pl.ds(keeps[part], half)] += ar[part, pl.ds(offset, half)]
            starts[part] = keeps[part]
        trail.append(keeps)
        offset += half
    piece = (length >> steps) // n_b

    def piece_at(part, index):
        return pl.ds(pl.multiple_of(starts[part] + index * piece, 8), piece)

    copies = []
    for part in range(parts):
        for d in range(1, n_b):
            target = band_at(d)
            copy = pltpu.make_async_remote_copy(
                src_ref=g.at[piece_at(part, target)],
                dst_ref=ar.at[part, pl.ds(offset + (d - 1) * piece, piece)],
                send_sem=z_send.at[0, d, part], recv_sem=z_recv.at[0, d, part],
                device_id=(s, target), device_id_type=MESH)
            copy.start()
            copies.append(copy)
    for copy in copies:
        copy.wait()
    copies = []
    for part in range(parts):
        own = piece_at(part, b)
        total = g[own]
        for d in range(1, n_b):
            total = total + ar[part, pl.ds(offset + (d - 1) * piece, piece)]
        whole[own] = total
        for d in range(1, n_b):
            copy = pltpu.make_async_remote_copy(
                src_ref=whole.at[own], dst_ref=whole.at[own],
                send_sem=z_send.at[1, d, part], recv_sem=z_recv.at[1, d, part],
                device_id=(s, band_at(d)), device_id_type=MESH)
            copy.start()
            copies.append(copy)
    for copy in copies:
        copy.wait()
    for k in reversed(range(steps)):
        half = length >> (k + 1)
        copies = []
        for part in range(parts):
            target, _ = partner(orders[part][k])
            keep = trail[k][part]
            copy = pltpu.make_async_remote_copy(
                src_ref=whole.at[pl.ds(keep, half)], dst_ref=whole.at[pl.ds(keep, half)],
                send_sem=ar_send.at[1, k, part], recv_sem=ar_recv.at[1, k, part],
                device_id=target, device_id_type=MESH)
            copy.start()
            copies.append(copy)
        for copy in copies:
            copy.wait()

    def gram_block(t):
        return jnp.concatenate(
            [whole[pl.ds((t * cuts + cut) * panel, panel)] for cut in range(cuts)], axis=1)

    eye = (lax.broadcasted_iota(jnp.int32, (panel, panel), 0)
           == lax.broadcasted_iota(jnp.int32, (panel, panel), 1))
    trace = sum(
        jnp.sum(jnp.where(eye, gram_block(pairs.index((i, i))), 0.0), keepdims=True)
        for i in range(n_b))
    scale = trace / vectors
    def put(i, j, value):
        columns = slice(j * panel, (j + 1) * panel)
        wh[i, :panel, columns], wl[i, :panel, columns] = split(value)

    for t, (i, j) in enumerate(pairs):
        normed = gram_block(t) / scale
        put(i, j, normed)
        if i != j:
            put(j, i, normed.T)

    def polynomial(i):
        high, low = wh[i, :panel, :vectors], wl[i, :panel, :vectors]
        matrix = tuple(ref[:n_b, :panel, :vectors].reshape(vectors, vectors) for ref in (wh, wl))
        squared = dot3((high, low), matrix)
        normed = high.astype(F32) + low.astype(F32)
        shape = (panel, vectors)
        row = lax.broadcasted_iota(jnp.int32, shape, 0) + i * panel
        diagonal = jnp.where(row == lax.broadcasted_iota(jnp.int32, shape, 1), 15.0, 0.0)
        return split(((diagonal - 10.0 * normed + 3.0 * squared) / 8.0).T)

    gain = jnp.sqrt(order / scale)

    def back(c, d):
        owner = band_at(d)
        return pltpu.make_async_remote_copy(
            src_ref=f1.at[rows_of(owner * per_home + c)],
            dst_ref=out.at[rows_of(b * per_home + c)],
            send_sem=back_send.at[c, d], recv_sem=back_recv.at[c, b],
            device_id=(s, owner), device_id_type=MESH)

    def own_back(c):
        at = rows_of(b * per_home + c)
        return pltpu.make_async_copy(f1.at[at], out.at[at], own_sem.at[c])

    def rotate(d, send):
        i = band_at(d)
        poly = polynomial(i)

        def rotate_rows(c, carry):
            left = tuple(
                jnp.concatenate([ref[rows_of(k * per_home + c)] for k in range(n_b)], axis=1)
                for ref in (xh, xl))
            f1[rows_of(i * per_home + c)] = dot3(left, poly) * gain
            send(c, d).start()
            return carry

        lax.fori_loop(0, per_home, rotate_rows, 0)

    for d in far_first:
        rotate(d, back)
    rotate(0, lambda c, d: own_back(c))

    def finish(c, carry):
        for d in range(1, n_b):
            to_home(c, d).wait_send()
            back(c, d).wait_send()
            source = band_at(d)
            pltpu.make_async_remote_copy(
                src_ref=f1.at[rows_of(c)],
                dst_ref=out.at[rows_of(source * per_home + c)],
                send_sem=back_send.at[c, d], recv_sem=back_recv.at[c, source],
                device_id=(s, source), device_id_type=MESH).wait_recv()
        own_back(c).wait()
        return carry

    lax.fori_loop(0, per_home, finish, 0)


def per_device(n_s, n_b, vectors, blocks, neighbours):
    elem, count, basis, _ = blocks.shape
    panel = vectors.shape[1]
    total = elem * n_s
    ids = lax.axis_index("space") * elem + jnp.arange(elem, dtype=jnp.int32)
    slots = (neighbours - ids[:, None] + REACH + total) % total
    weights = jax.nn.one_hot(slots, SPAN, dtype=F32).reshape(-1)

    rows = elem * basis
    per_home = elem // n_b
    devices = n_s * n_b
    need = n_b * (n_b + 1) // 2 * (panel // LANES) * panel
    parts = 2 if need % (16 * devices) == 0 else 1
    unit = 8 * devices * parts
    packed = -(-need // unit) * unit
    steps = n_s.bit_length() - 1
    padded = (elem + 2 * REACH) * basis
    dma = pltpu.SemaphoreType.DMA
    any_spec = pl.BlockSpec(memory_space=pl.ANY)
    flops = 2 * rows * panel * 3 * (2 * SPAN * basis) + 6 * rows * panel * 1024 * 3
    return pl.pallas_call(
        functools.partial(main_kernel, n_s, n_b, elem, basis, panel, parts),
        out_shape=jax.ShapeDtypeStruct((rows, panel), F32),
        in_specs=[pl.BlockSpec(memory_space=pltpu.SMEM), any_spec, any_spec],
        out_specs=any_spec,
        scratch_shapes=[
            pltpu.VMEM((rows, panel), F32),
            pltpu.VMEM((padded, panel), BF16),
            pltpu.VMEM((padded, panel), BF16),
            pltpu.VMEM((padded, panel), BF16),
            pltpu.VMEM((padded, panel), BF16),
            pltpu.VMEM((elem, basis, SPAN * basis), BF16),
            pltpu.VMEM((elem, basis, SPAN * basis), BF16),
            pltpu.VMEM((rows, panel), F32),
            pltpu.VMEM((rows, panel), F32),
            pltpu.VMEM((packed, LANES), F32),
            pltpu.VMEM((parts, packed // parts, LANES), F32),
            pltpu.VMEM((packed, LANES), F32),
            pltpu.VMEM((2, 2, REACH * basis, panel), F32),
            pltpu.VMEM((3, count, basis, basis), F32),
            dma, dma((3,)), dma((2, 2)), dma((2, 2)),
            dma((per_home, n_b)), dma((per_home, n_b)),
            dma((2, steps, parts)), dma((2, steps, parts)),
            dma((2, n_b, parts)), dma((2, n_b, parts)),
            dma((per_home, n_b)), dma((per_home, n_b)), dma((per_home,)),
        ],
        compiler_params=pltpu.CompilerParams(
            collective_id=0, has_side_effects=True, vmem_limit_bytes=60 * 2**20),
        cost_estimate=pl.CostEstimate(
            flops=flops, bytes_accessed=40 * 2**20, transcendentals=0),
        name="filter_and_rotate",
    )(weights, vectors, blocks)


def solution(mesh):
    return jax.shard_map(
        functools.partial(per_device, mesh.shape["space"], mesh.shape["band"]),
        mesh=mesh,
        in_specs=(P("space", "band"), P("space", None, None, None), P("space", None)),
        out_specs=P("space", "band"),
        check_vma=False,
    )
```

```python
import functools

import jax
import jax.numpy as jnp
from jax import lax
from jax.experimental import pallas as pl
from jax.experimental.pallas import tpu as pltpu
from jax.sharding import PartitionSpec as P

REACH = 2
SPAN = 2 * REACH + 1
LANES = 128
MESH = pl.DeviceIdType.MESH
F32 = jnp.float32
BF16 = jnp.bfloat16


def split(x):
    high = x.astype(BF16)
    return high, (x - high.astype(F32)).astype(BF16)


def dot3(a, b):
    (ah, al), (bh, bl) = a, b
    mul = functools.partial(jnp.dot, preferred_element_type=F32)
    return mul(ah, bh) + (mul(ah, bl) + mul(al, bh))


def main_kernel(
    n_s, n_b, elem, basis, panel, parts,
    weights, v_hbm, blocks, out,
    x, xh, xl, fh, fl, wh, wl, f1, recv, g, ar, whole, halo, raw, dsum, dar, dwhole,
    load_sem, raw_sem, halo_send, halo_recv, a2a_send, a2a_recv, ar_send, ar_recv,
    z_send, z_recv, d_send, d_recv, dz_send, dz_recv,
    back_send, back_recv, own_sem,
):
    s, b = lax.axis_index("space"), lax.axis_index("band")
    per_home = elem // n_b
    home_rows = per_home * basis
    edge = REACH * basis
    vectors = n_b * panel
    order = n_s * elem * basis
    up, down = lax.rem(s + 1, n_s), lax.rem(s + n_s - 1, n_s)

    def rows_of(e):
        return pl.ds(pl.multiple_of(e * basis, basis), basis)

    def band_at(d):
        return lax.rem(b + d, n_b)

    def xor(index, bit):
        return index + bit * (1 - 2 * lax.rem(index // bit, 2))

    space_bits = [1 << k for k in range(n_s.bit_length() - 1)]
    loads = [pltpu.make_async_copy(v_hbm, x, load_sem)]
    loads[0].start()

    count, slots = blocks.shape[1], raw.shape[0]

    def element_at(p):
        return lax.rem(p + elem // 2, elem)

    def raw_copy(p):
        slot = lax.rem(p, slots)
        return pltpu.make_async_copy(blocks.at[element_at(p)], raw.at[slot], raw_sem.at[slot])

    for p in range(slots - 1):
        raw_copy(jnp.int32(p)).start()

    barrier = pltpu.get_barrier_semaphore()
    peers = [(up, b), (down, b)]
    peers += [(s, band_at(d)) for d in range(1, n_b)]
    peers += [(xor(s, bit), b) for bit in space_bits]
    for peer in peers:
        pl.semaphore_signal(barrier, inc=1, device_id=peer, device_id_type=MESH)
    pl.semaphore_wait(barrier, len(peers))

    def halo_copies(step, field):
        def copy(src, side, target):
            return pltpu.make_async_remote_copy(
                src_ref=src, dst_ref=halo.at[step, side],
                send_sem=halo_send.at[step, side], recv_sem=halo_recv.at[step, side],
                device_id=(target, b), device_id_type=MESH)
        last = field.at[pl.ds(elem * basis - edge, edge)]
        first = field.at[pl.ds(0, edge)]
        return copy(last, 0, up), copy(first, 1, down)

    def take_halo(step, copies, high, low):
        for side, copy in enumerate(copies):
            copy.wait_recv()
            start = side * (elem + REACH) * basis
            high[pl.ds(start, edge)], low[pl.ds(start, edge)] = split(halo[step, side])

    def applied(e, high, low):
        near = pl.ds(pl.multiple_of(e * basis, basis), SPAN * basis)
        return dot3((wh[e], wl[e]), (high[near], low[near]))

    loads[0].wait()
    halo1 = halo_copies(0, x)
    for copy in halo1:
        copy.start()

    def split_x(e, carry):
        at = rows_of(e + REACH)
        xh[at], xl[at] = split(x[rows_of(e)])
        return carry

    lax.fori_loop(0, elem, split_x, 0)

    tile = 32

    def merge(p, e):
        raw_copy(p).wait()

        @pl.when(p + slots - 1 < elem)
        def _():
            raw_copy(p + slots - 1).start()

        slot = lax.rem(p, slots)
        weight = [
            [weights[(e * count + k) * SPAN + o] for o in range(SPAN)] for k in range(count)]

        def merge_rows(r, carry):
            at = pl.ds(pl.multiple_of(r * tile, tile), tile)
            blocks_at = [raw[slot, k, at, :] for k in range(count)]
            for o in range(SPAN):
                total = {0: blocks_at[1], SPAN - 1: blocks_at[2]}.get(o)
                for k in range(count):
                    if k not in (1, 2):
                        term = blocks_at[k] * weight[k][o]
                        total = term if total is None else total + term
                columns = slice(o * basis, (o + 1) * basis)
                wh[e, at, columns], wl[e, at, columns] = split(total)
            return carry

        lax.fori_loop(0, basis // tile, merge_rows, 0)

    def first_apply(p, carry):
        e = element_at(p)
        merge(p, e)
        value = (applied(e, xh, xl) - 0.5 * x[rows_of(e)]) / 1.5
        f1[rows_of(e)] = value
        at = rows_of(e + REACH)
        fh[at], fl[at] = split(value)
        return carry

    lax.fori_loop(0, elem // 2 - REACH, first_apply, 0)
    take_halo(0, halo1, xh, xl)
    lax.fori_loop(elem // 2 - REACH, elem // 2 + REACH, first_apply, 0)
    halo2 = halo_copies(1, f1)
    for copy in halo2:
        copy.start()
    lax.fori_loop(elem // 2 + REACH, elem, first_apply, 0)
    for copy in halo1:
        copy.wait_send()
    take_halo(1, halo2, fh, fl)

    def filtered_of(e):
        mine = rows_of(e)
        return 2.0 * (applied(e, fh, fl) - 0.5 * f1[mine]) / 1.5 - x[mine]

    def to_home(c, d):
        home = band_at(d)
        return pltpu.make_async_remote_copy(
            src_ref=x.at[rows_of(home * per_home + c)],
            dst_ref=recv.at[rows_of(b * per_home + c)],
            send_sem=a2a_send.at[c, d], recv_sem=a2a_recv.at[c, b],
            device_id=(s, home), device_id_type=MESH)

    far_first = sorted(range(1, n_b), key=lambda d: -min(d, n_b - d))

    def second_apply(c, carry):
        for d in far_first:
            e = band_at(d) * per_home + c
            x[rows_of(e)] = filtered_of(e)
            to_home(c, d).start()
        e = b * per_home + c
        value = filtered_of(e)
        x[rows_of(e)] = value
        recv[rows_of(e)] = value
        return carry

    lax.fori_loop(0, per_home, second_apply, 0)
    for copy in halo2:
        copy.wait_send()

    cuts = panel // LANES

    def partner(bit):
        return (xor(s, bit), b), lax.rem(s // bit, 2)

    def unpacked(ref, first):
        return jnp.concatenate(
            [ref[pl.ds((first + cut) * panel, panel)] for cut in range(cuts)], axis=1)

    dsum[...] = jnp.zeros_like(dsum)

    def add_own(e, carry):
        value = x[rows_of(e)]
        product = dot3(split(value.T), split(value))
        for cut in range(cuts):
            dsum[pl.ds(cut * panel, panel)] += product[:, cut * LANES:(cut + 1) * LANES]
        return carry

    lax.fori_loop(0, elem, add_own, 0)
    own_start, own_half, own_trail, offset = 0, dsum.shape[0], [], 0
    for k, space_bit in enumerate(space_bits):
        own_half //= 2
        target, bit = partner(space_bit)
        keep = pl.multiple_of(own_start + bit * own_half, 8)
        give = pl.multiple_of(own_start + (1 - bit) * own_half, 8)
        copy = pltpu.make_async_remote_copy(
            src_ref=dsum.at[pl.ds(give, own_half)], dst_ref=dar.at[pl.ds(offset, own_half)],
            send_sem=d_send.at[0, k], recv_sem=d_recv.at[0, k],
            device_id=target, device_id_type=MESH)
        copy.start()
        copy.wait()
        dsum[pl.ds(keep, own_half)] += dar[pl.ds(offset, own_half)]
        own_start = keep
        own_trail.append((keep, own_half))
        offset += own_half
    own_piece = pl.ds(own_start, own_half)
    dwhole[b, own_piece] = dsum[own_piece]
    copies = []
    for d in range(1, n_b):
        copy = pltpu.make_async_remote_copy(
            src_ref=dwhole.at[b, own_piece], dst_ref=dwhole.at[b, own_piece],
            send_sem=dz_send.at[d], recv_sem=dz_recv.at[d],
            device_id=(s, band_at(d)), device_id_type=MESH)
        copy.start()
        copies.append(copy)
    for copy in copies:
        copy.wait()
    for k in reversed(range(len(space_bits))):
        target, _ = partner(space_bits[k])
        held = pl.ds(*own_trail[k])
        copy = pltpu.make_async_remote_copy(
            src_ref=dwhole.at[:, held], dst_ref=dwhole.at[:, held],
            send_sem=d_send.at[1, k], recv_sem=d_recv.at[1, k],
            device_id=target, device_id_type=MESH)
        copy.start()
        copy.wait()

    eye = (lax.broadcasted_iota(jnp.int32, (panel, panel), 0)
           == lax.broadcasted_iota(jnp.int32, (panel, panel), 1))
    trace = sum(
        jnp.sum(jnp.where(eye, unpacked(dwhole.at[i], 0), 0.0), keepdims=True)
        for i in range(n_b))
    scale = trace / vectors

    def put(i, j, value):
        columns = slice(j * panel, (j + 1) * panel)
        wh[i, :panel, columns], wl[i, :panel, columns] = split(value)

    for i in range(n_b):
        put(i, i, unpacked(dwhole.at[i], 0) / scale)

    pairs = [(i, j) for i in range(n_b) for j in range(i + 1, n_b)]
    g[...] = jnp.zeros_like(g)

    def from_home(c, d):
        source = band_at(d)
        return pltpu.make_async_remote_copy(
            src_ref=x.at[rows_of(c)],
            dst_ref=recv.at[rows_of(source * per_home + c)],
            send_sem=a2a_send.at[c, d], recv_sem=a2a_recv.at[c, source],
            device_id=(s, source), device_id_type=MESH)

    def add_gram(c, carry):
        for d in range(1, n_b):
            from_home(c, d).wait_recv()
        parts_of = []
        for i in range(n_b):
            at = rows_of(i * per_home + c)
            high, low = split(recv[at])
            xh[at], xl[at] = high, low
            parts_of.append((high, low))
        for i in range(n_b - 1):
            turned = split(recv[rows_of(i * per_home + c)].T)
            for j in range(i + 1, n_b):
                product = dot3(turned, parts_of[j])
                t = pairs.index((i, j))
                for cut in range(cuts):
                    g[pl.ds((t * cuts + cut) * panel, panel)] += product[:, cut * LANES:(cut + 1) * LANES]
        return carry

    lax.fori_loop(0, per_home, add_gram, 0)

    length = g.shape[0] // parts
    orders = [
        space_bits[:1] + (space_bits[1:][::-1] if part % 2 else space_bits[1:])
        for part in range(parts)]
    steps = len(space_bits)

    starts = [part * length for part in range(parts)]
    trail = []
    offset = 0
    for k in range(steps):
        half = length >> (k + 1)
        copies, keeps = [], []
        for part in range(parts):
            target, bit = partner(orders[part][k])
            keep = pl.multiple_of(starts[part] + bit * half, 8)
            give = pl.multiple_of(starts[part] + (1 - bit) * half, 8)
            copy = pltpu.make_async_remote_copy(
                src_ref=g.at[pl.ds(give, half)], dst_ref=ar.at[part, pl.ds(offset, half)],
                send_sem=ar_send.at[0, k, part], recv_sem=ar_recv.at[0, k, part],
                device_id=target, device_id_type=MESH)
            copy.start()
            copies.append(copy)
            keeps.append(keep)
        for part in range(parts):
            copies[part].wait()
            g[pl.ds(keeps[part], half)] += ar[part, pl.ds(offset, half)]
            starts[part] = keeps[part]
        trail.append(keeps)
        offset += half
    piece = (length >> steps) // n_b

    def piece_at(part, index):
        return pl.ds(pl.multiple_of(starts[part] + index * piece, 8), piece)

    copies = []
    for part in range(parts):
        for d in range(1, n_b):
            target = band_at(d)
            copy = pltpu.make_async_remote_copy(
                src_ref=g.at[piece_at(part, target)],
                dst_ref=ar.at[part, pl.ds(offset + (d - 1) * piece, piece)],
                send_sem=z_send.at[0, d, part], recv_sem=z_recv.at[0, d, part],
                device_id=(s, target), device_id_type=MESH)
            copy.start()
            copies.append(copy)
    for copy in copies:
        copy.wait()
    copies = []
    for part in range(parts):
        own = piece_at(part, b)
        total = g[own]
        for d in range(1, n_b):
            total = total + ar[part, pl.ds(offset + (d - 1) * piece, piece)]
        whole[own] = total
        for d in range(1, n_b):
            copy = pltpu.make_async_remote_copy(
                src_ref=whole.at[own], dst_ref=whole.at[own],
                send_sem=z_send.at[1, d, part], recv_sem=z_recv.at[1, d, part],
                device_id=(s, band_at(d)), device_id_type=MESH)
            copy.start()
            copies.append(copy)
    for copy in copies:
        copy.wait()
    for k in reversed(range(steps)):
        half = length >> (k + 1)
        copies = []
        for part in range(parts):
            target, _ = partner(orders[part][k])
            keep = trail[k][part]
            copy = pltpu.make_async_remote_copy(
                src_ref=whole.at[pl.ds(keep, half)], dst_ref=whole.at[pl.ds(keep, half)],
                send_sem=ar_send.at[1, k, part], recv_sem=ar_recv.at[1, k, part],
                device_id=target, device_id_type=MESH)
            copy.start()
            copies.append(copy)
        for copy in copies:
            copy.wait()

    for t, (i, j) in enumerate(pairs):
        normed = unpacked(whole, t * cuts) / scale
        put(i, j, normed)
        put(j, i, normed.T)

    def polynomial(i):
        high, low = wh[i, :panel, :vectors], wl[i, :panel, :vectors]
        matrix = tuple(ref[:n_b, :panel, :vectors].reshape(vectors, vectors) for ref in (wh, wl))
        squared = dot3((high, low), matrix)
        normed = high.astype(F32) + low.astype(F32)
        shape = (panel, vectors)
        row = lax.broadcasted_iota(jnp.int32, shape, 0) + i * panel
        diagonal = jnp.where(row == lax.broadcasted_iota(jnp.int32, shape, 1), 15.0, 0.0)
        return split(((diagonal - 10.0 * normed + 3.0 * squared) / 8.0).T)

    gain = jnp.sqrt(order / scale)

    def back(c, d):
        owner = band_at(d)
        return pltpu.make_async_remote_copy(
            src_ref=f1.at[rows_of(owner * per_home + c)],
            dst_ref=out.at[rows_of(b * per_home + c)],
            send_sem=back_send.at[c, d], recv_sem=back_recv.at[c, b],
            device_id=(s, owner), device_id_type=MESH)

    def own_back(c):
        at = rows_of(b * per_home + c)
        return pltpu.make_async_copy(f1.at[at], out.at[at], own_sem.at[c])

    def rotate(d, send):
        i = band_at(d)
        poly = polynomial(i)

        def rotate_rows(c, carry):
            left = tuple(
                jnp.concatenate([ref[rows_of(k * per_home + c)] for k in range(n_b)], axis=1)
                for ref in (xh, xl))
            f1[rows_of(i * per_home + c)] = dot3(left, poly) * gain
            send(c, d).start()
            return carry

        lax.fori_loop(0, per_home, rotate_rows, 0)

    for d in far_first:
        rotate(d, back)
    rotate(0, lambda c, d: own_back(c))

    def finish(c, carry):
        for d in range(1, n_b):
            to_home(c, d).wait_send()
            back(c, d).wait_send()
            source = band_at(d)
            pltpu.make_async_remote_copy(
                src_ref=f1.at[rows_of(c)],
                dst_ref=out.at[rows_of(source * per_home + c)],
                send_sem=back_send.at[c, d], recv_sem=back_recv.at[c, source],
                device_id=(s, source), device_id_type=MESH).wait_recv()
        own_back(c).wait()
        return carry

    lax.fori_loop(0, per_home, finish, 0)


def per_device(n_s, n_b, vectors, blocks, neighbours):
    elem, count, basis, _ = blocks.shape
    panel = vectors.shape[1]
    total = elem * n_s
    ids = lax.axis_index("space") * elem + jnp.arange(elem, dtype=jnp.int32)
    slots = (neighbours - ids[:, None] + REACH + total) % total
    weights = jax.nn.one_hot(slots, SPAN, dtype=F32).reshape(-1)

    rows = elem * basis
    per_home = elem // n_b
    devices = n_s * n_b
    block_rows = panel // LANES * panel
    need = n_b * (n_b - 1) // 2 * block_rows
    parts = 2 if need % (16 * devices) == 0 else 1
    unit = 8 * devices * parts
    packed = -(-need // unit) * unit
    steps = n_s.bit_length() - 1
    padded = (elem + 2 * REACH) * basis
    dma = pltpu.SemaphoreType.DMA
    any_spec = pl.BlockSpec(memory_space=pl.ANY)
    flops = 2 * rows * panel * 3 * (2 * SPAN * basis) + 6 * rows * panel * 1024 * 3
    return pl.pallas_call(
        functools.partial(main_kernel, n_s, n_b, elem, basis, panel, parts),
        out_shape=jax.ShapeDtypeStruct((rows, panel), F32),
        in_specs=[pl.BlockSpec(memory_space=pltpu.SMEM), any_spec, any_spec],
        out_specs=any_spec,
        scratch_shapes=[
            pltpu.VMEM((rows, panel), F32),
            pltpu.VMEM((padded, panel), BF16),
            pltpu.VMEM((padded, panel), BF16),
            pltpu.VMEM((padded, panel), BF16),
            pltpu.VMEM((padded, panel), BF16),
            pltpu.VMEM((elem, basis, SPAN * basis), BF16),
            pltpu.VMEM((elem, basis, SPAN * basis), BF16),
            pltpu.VMEM((rows, panel), F32),
            pltpu.VMEM((rows, panel), F32),
            pltpu.VMEM((packed, LANES), F32),
            pltpu.VMEM((parts, packed // parts, LANES), F32),
            pltpu.VMEM((packed, LANES), F32),
            pltpu.VMEM((2, 2, REACH * basis, panel), F32),
            pltpu.VMEM((3, count, basis, basis), F32),
            pltpu.VMEM((block_rows, LANES), F32),
            pltpu.VMEM((block_rows, LANES), F32),
            pltpu.VMEM((n_b, block_rows, LANES), F32),
            dma, dma((3,)), dma((2, 2)), dma((2, 2)),
            dma((per_home, n_b)), dma((per_home, n_b)),
            dma((2, steps, parts)), dma((2, steps, parts)),
            dma((2, n_b, parts)), dma((2, n_b, parts)),
            dma((2, steps)), dma((2, steps)), dma((n_b,)), dma((n_b,)),
            dma((per_home, n_b)), dma((per_home, n_b)), dma((per_home,)),
        ],
        compiler_params=pltpu.CompilerParams(
            collective_id=0, has_side_effects=True, vmem_limit_bytes=60 * 2**20),
        cost_estimate=pl.CostEstimate(
            flops=flops, bytes_accessed=40 * 2**20, transcendentals=0),
        name="filter_and_rotate",
    )(weights, vectors, blocks)


def solution(mesh):
    return jax.shard_map(
        functools.partial(per_device, mesh.shape["space"], mesh.shape["band"]),
        mesh=mesh,
        in_specs=(P("space", "band"), P("space", None, None, None), P("space", None)),
        out_specs=P("space", "band"),
        check_vma=False,
    )
```

```python
import functools

import jax
import jax.numpy as jnp
from jax import lax
from jax.experimental import pallas as pl
from jax.experimental.pallas import tpu as pltpu
from jax.sharding import PartitionSpec as P

REACH = 2
SPAN = 2 * REACH + 1
LANES = 128
MESH = pl.DeviceIdType.MESH
F32 = jnp.float32
BF16 = jnp.bfloat16


def split(x):
    high = x.astype(BF16)
    return high, (x - high.astype(F32)).astype(BF16)


def dot3(a, b):
    (ah, al), (bh, bl) = a, b
    mul = functools.partial(jnp.dot, preferred_element_type=F32)
    return mul(ah, bh) + (mul(ah, bl) + mul(al, bh))


def main_kernel(
    n_s, n_b, elem, basis, panel, parts,
    weights, v_hbm, blocks, out,
    x, xh, xl, fh, fl, wh, wl, f1, recv, g, ar, whole, halo, raw, dsum, dar, dwhole,
    load_sem, raw_sem, halo_send, halo_recv, a2a_send, a2a_recv, ar_send, ar_recv,
    z_send, z_recv, d_send, d_recv, dz_send, dz_recv,
    back_send, back_recv, own_sem,
):
    s, b = lax.axis_index("space"), lax.axis_index("band")
    per_home = elem // n_b
    home_rows = per_home * basis
    edge = REACH * basis
    vectors = n_b * panel
    order = n_s * elem * basis
    up, down = lax.rem(s + 1, n_s), lax.rem(s + n_s - 1, n_s)

    def rows_of(e):
        return pl.ds(pl.multiple_of(e * basis, basis), basis)

    def band_at(d):
        return lax.rem(b + d, n_b)

    def xor(index, bit):
        return index + bit * (1 - 2 * lax.rem(index // bit, 2))

    space_bits = [1 << k for k in range(n_s.bit_length() - 1)]
    loads = [pltpu.make_async_copy(v_hbm, x, load_sem)]
    loads[0].start()

    count, slots = blocks.shape[1], raw.shape[0]

    def element_at(p):
        return lax.rem(p + elem // 2, elem)

    def raw_copy(p):
        slot = lax.rem(p, slots)
        return pltpu.make_async_copy(blocks.at[element_at(p)], raw.at[slot], raw_sem.at[slot])

    for p in range(slots - 1):
        raw_copy(jnp.int32(p)).start()

    barrier = pltpu.get_barrier_semaphore()
    peers = [(up, b), (down, b)]
    peers += [(s, band_at(d)) for d in range(1, n_b)]
    peers += [(xor(s, bit), b) for bit in space_bits]
    for peer in peers:
        pl.semaphore_signal(barrier, inc=1, device_id=peer, device_id_type=MESH)
    pl.semaphore_wait(barrier, len(peers))

    def halo_copies(step, field):
        def copy(src, side, target):
            return pltpu.make_async_remote_copy(
                src_ref=src, dst_ref=halo.at[step, side],
                send_sem=halo_send.at[step, side], recv_sem=halo_recv.at[step, side],
                device_id=(target, b), device_id_type=MESH)
        last = field.at[pl.ds(elem * basis - edge, edge)]
        first = field.at[pl.ds(0, edge)]
        return copy(last, 0, up), copy(first, 1, down)

    def take_halo(step, copies, high, low):
        for side, copy in enumerate(copies):
            copy.wait_recv()
            start = side * (elem + REACH) * basis
            high[pl.ds(start, edge)], low[pl.ds(start, edge)] = split(halo[step, side])

    def applied(e, high, low):
        near = pl.ds(pl.multiple_of(e * basis, basis), SPAN * basis)
        return dot3((wh[e], wl[e]), (high[near], low[near]))

    loads[0].wait()
    halo1 = halo_copies(0, x)
    for copy in halo1:
        copy.start()

    def split_x(e, carry):
        at = rows_of(e + REACH)
        xh[at], xl[at] = split(x[rows_of(e)])
        return carry

    lax.fori_loop(0, elem, split_x, 0)

    tile = 32

    def merge(p, e):
        raw_copy(p).wait()

        @pl.when(p + slots - 1 < elem)
        def _():
            raw_copy(p + slots - 1).start()

        slot = lax.rem(p, slots)
        weight = [
            [weights[(e * count + k) * SPAN + o] for o in range(SPAN)] for k in range(count)]

        def merge_rows(r, carry):
            at = pl.ds(pl.multiple_of(r * tile, tile), tile)
            blocks_at = [raw[slot, k, at, :] for k in range(count)]
            for o in range(SPAN):
                total = {0: blocks_at[1], SPAN - 1: blocks_at[2]}.get(o)
                for k in range(count):
                    if k not in (1, 2):
                        term = blocks_at[k] * weight[k][o]
                        total = term if total is None else total + term
                columns = slice(o * basis, (o + 1) * basis)
                wh[e, at, columns], wl[e, at, columns] = split(total)
            return carry

        lax.fori_loop(0, basis // tile, merge_rows, 0)

    def first_apply(p, carry):
        e = element_at(p)
        merge(p, e)
        value = (applied(e, xh, xl) - 0.5 * x[rows_of(e)]) / 1.5
        f1[rows_of(e)] = value
        at = rows_of(e + REACH)
        fh[at], fl[at] = split(value)
        return carry

    lax.fori_loop(0, elem // 2 - REACH, first_apply, 0)
    take_halo(0, halo1, xh, xl)
    lax.fori_loop(elem // 2 - REACH, elem // 2 + REACH, first_apply, 0)
    halo2 = halo_copies(1, f1)
    for copy in halo2:
        copy.start()
    lax.fori_loop(elem // 2 + REACH, elem, first_apply, 0)
    for copy in halo1:
        copy.wait_send()
    take_halo(1, halo2, fh, fl)

    def filtered_of(e):
        mine = rows_of(e)
        return 2.0 * (applied(e, fh, fl) - 0.5 * f1[mine]) / 1.5 - x[mine]

    def to_home(c, d):
        home = band_at(d)
        return pltpu.make_async_remote_copy(
            src_ref=x.at[rows_of(home * per_home + c)],
            dst_ref=recv.at[rows_of(b * per_home + c)],
            send_sem=a2a_send.at[c, d], recv_sem=a2a_recv.at[c, b],
            device_id=(s, home), device_id_type=MESH)

    far_first = sorted(range(1, n_b), key=lambda d: -min(d, n_b - d))

    def second_apply(c, carry):
        for d in far_first:
            e = band_at(d) * per_home + c
            x[rows_of(e)] = filtered_of(e)
            if carry:
                to_home(c, d).start()
        e = b * per_home + c
        value = filtered_of(e)
        x[rows_of(e)] = value
        recv[rows_of(e)] = value

    def send_chunks(first, last):
        for c in range(first, last):
            for d in far_first:
                to_home(c, d).start()

    early = per_home // 2
    middle = early + (per_home - early) // 2
    pl.loop(0, early)(lambda c: second_apply(c, True))
    pl.loop(early, per_home)(lambda c: second_apply(c, False))
    for copy in halo2:
        copy.wait_send()

    cuts = panel // LANES

    def partner(bit):
        return (xor(s, bit), b), lax.rem(s // bit, 2)

    def unpacked(ref, first):
        return jnp.concatenate(
            [ref[pl.ds((first + cut) * panel, panel)] for cut in range(cuts)], axis=1)

    pairs = [(i, j) for i in range(n_b) for j in range(i + 1, n_b)]
    g[...] = jnp.zeros_like(g)

    def from_home(c, d):
        source = band_at(d)
        return pltpu.make_async_remote_copy(
            src_ref=x.at[rows_of(c)],
            dst_ref=recv.at[rows_of(source * per_home + c)],
            send_sem=a2a_send.at[c, d], recv_sem=a2a_recv.at[c, source],
            device_id=(s, source), device_id_type=MESH)

    def add_gram(c, carry):
        for d in range(1, n_b):
            from_home(c, d).wait_recv()
        parts_of = []
        for i in range(n_b):
            at = rows_of(i * per_home + c)
            high, low = split(recv[at])
            xh[at], xl[at] = high, low
            parts_of.append((high, low))
        for i in range(n_b - 1):
            turned = split(recv[rows_of(i * per_home + c)].T)
            for j in range(i + 1, n_b):
                product = dot3(turned, parts_of[j])
                t = pairs.index((i, j))
                for cut in range(cuts):
                    g[pl.ds((t * cuts + cut) * panel, panel)] += product[:, cut * LANES:(cut + 1) * LANES]
        return carry

    dsum[...] = jnp.zeros_like(dsum)

    def add_own(e, carry):
        value = x[rows_of(e)]
        product = dot3(split(value.T), split(value))
        for cut in range(cuts):
            dsum[pl.ds(cut * panel, panel)] += product[:, cut * LANES:(cut + 1) * LANES]
        return carry

    lax.fori_loop(0, elem, add_own, 0)
    own_start, own_half, own_trail, offset = 0, dsum.shape[0], [], 0
    for k, space_bit in enumerate(space_bits):
        own_half //= 2
        target, bit = partner(space_bit)
        keep = pl.multiple_of(own_start + bit * own_half, 8)
        give = pl.multiple_of(own_start + (1 - bit) * own_half, 8)
        copy = pltpu.make_async_remote_copy(
            src_ref=dsum.at[pl.ds(give, own_half)], dst_ref=dar.at[pl.ds(offset, own_half)],
            send_sem=d_send.at[0, k], recv_sem=d_recv.at[0, k],
            device_id=target, device_id_type=MESH)
        copy.start()
        if k == 0:
            send_chunks(early, middle)
        if k == 1:
            send_chunks(middle, per_home)
        if k == len(space_bits) - 1:
            lax.fori_loop(0, per_home - 1, add_gram, 0)
        copy.wait()
        dsum[pl.ds(keep, own_half)] += dar[pl.ds(offset, own_half)]
        own_start = keep
        own_trail.append((keep, own_half))
        offset += own_half
    own_piece = pl.ds(own_start, own_half)
    dwhole[b, own_piece] = dsum[own_piece]
    own_copies = []
    for d in range(1, n_b):
        copy = pltpu.make_async_remote_copy(
            src_ref=dwhole.at[b, own_piece], dst_ref=dwhole.at[b, own_piece],
            send_sem=dz_send.at[d], recv_sem=dz_recv.at[d],
            device_id=(s, band_at(d)), device_id_type=MESH)
        copy.start()
        own_copies.append(copy)
    add_gram(per_home - 1, 0)

    length = g.shape[0] // parts
    orders = [
        space_bits[:1] + (space_bits[1:][::-1] if part % 2 else space_bits[1:])
        for part in range(parts)]
    steps = len(space_bits)

    starts = [part * length for part in range(parts)]
    trail = []
    offset = 0

    def halve(part, k, offset):
        half = length >> (k + 1)
        target, bit = partner(orders[part][k])
        keep = pl.multiple_of(starts[part] + bit * half, 8)
        give = pl.multiple_of(starts[part] + (1 - bit) * half, 8)
        copy = pltpu.make_async_remote_copy(
            src_ref=g.at[pl.ds(give, half)], dst_ref=ar.at[part, pl.ds(offset, half)],
            send_sem=ar_send.at[0, k, part], recv_sem=ar_recv.at[0, k, part],
            device_id=target, device_id_type=MESH)
        copy.start()
        return copy, keep

    current = [halve(part, 0, 0) for part in range(parts)]
    halved = []
    for k in range(steps):
        half = length >> (k + 1)
        trail.append([keep for _, keep in current])
        for part, (copy, keep) in enumerate(current):
            copy.wait_recv()
            halved.append(copy)
            g[pl.ds(keep, half)] += ar[part, pl.ds(offset, half)]
            starts[part] = keep
            if k + 1 < steps:
                current[part] = halve(part, k + 1, offset + half)
        offset += half
    for copy in halved:
        copy.wait_send()
    piece = (length >> steps) // n_b

    def piece_at(part, index):
        return pl.ds(pl.multiple_of(starts[part] + index * piece, 8), piece)

    copies = []
    for part in range(parts):
        for d in range(1, n_b):
            target = band_at(d)
            copy = pltpu.make_async_remote_copy(
                src_ref=g.at[piece_at(part, target)],
                dst_ref=ar.at[part, pl.ds(offset + (d - 1) * piece, piece)],
                send_sem=z_send.at[0, d, part], recv_sem=z_recv.at[0, d, part],
                device_id=(s, target), device_id_type=MESH)
            copy.start()
            copies.append(copy)
    for copy in copies:
        copy.wait()
    copies = []
    for part in range(parts):
        own = piece_at(part, b)
        total = g[own]
        for d in range(1, n_b):
            total = total + ar[part, pl.ds(offset + (d - 1) * piece, piece)]
        whole[own] = total
        for d in range(1, n_b):
            copy = pltpu.make_async_remote_copy(
                src_ref=whole.at[own], dst_ref=whole.at[own],
                send_sem=z_send.at[1, d, part], recv_sem=z_recv.at[1, d, part],
                device_id=(s, band_at(d)), device_id_type=MESH)
            copy.start()
            copies.append(copy)
    for copy in copies + own_copies:
        copy.wait()
    for k in reversed(range(steps)):
        half = length >> (k + 1)
        target, _ = partner(space_bits[k])
        held = pl.ds(*own_trail[k])
        copy = pltpu.make_async_remote_copy(
            src_ref=dwhole.at[:, held], dst_ref=dwhole.at[:, held],
            send_sem=d_send.at[1, k], recv_sem=d_recv.at[1, k],
            device_id=target, device_id_type=MESH)
        copy.start()
        copies = [copy]
        for part in range(parts):
            target, _ = partner(orders[part][k])
            keep = trail[k][part]
            copy = pltpu.make_async_remote_copy(
                src_ref=whole.at[pl.ds(keep, half)], dst_ref=whole.at[pl.ds(keep, half)],
                send_sem=ar_send.at[1, k, part], recv_sem=ar_recv.at[1, k, part],
                device_id=target, device_id_type=MESH)
            copy.start()
            copies.append(copy)
        for copy in copies:
            copy.wait()

    eye = (lax.broadcasted_iota(jnp.int32, (panel, panel), 0)
           == lax.broadcasted_iota(jnp.int32, (panel, panel), 1))
    trace = sum(
        jnp.sum(jnp.where(eye, unpacked(dwhole.at[i], 0), 0.0), keepdims=True)
        for i in range(n_b))
    scale = trace / vectors

    def put(i, j, value):
        columns = slice(j * panel, (j + 1) * panel)
        wh[i, :panel, columns], wl[i, :panel, columns] = split(value)

    for i in range(n_b):
        put(i, i, unpacked(dwhole.at[i], 0) / scale)

    for t, (i, j) in enumerate(pairs):
        normed = unpacked(whole, t * cuts) / scale
        put(i, j, normed)
        put(j, i, normed.T)

    def polynomial(i):
        high, low = wh[i, :panel, :vectors], wl[i, :panel, :vectors]
        matrix = tuple(ref[:n_b, :panel, :vectors].reshape(vectors, vectors) for ref in (wh, wl))
        squared = dot3((high, low), matrix)
        normed = high.astype(F32) + low.astype(F32)
        shape = (panel, vectors)
        row = lax.broadcasted_iota(jnp.int32, shape, 0) + i * panel
        diagonal = jnp.where(row == lax.broadcasted_iota(jnp.int32, shape, 1), 15.0, 0.0)
        return split(((diagonal - 10.0 * normed + 3.0 * squared) / 8.0).T)

    gain = jnp.sqrt(order / scale)

    def back(c, d):
        owner = band_at(d)
        return pltpu.make_async_remote_copy(
            src_ref=f1.at[rows_of(owner * per_home + c)],
            dst_ref=out.at[rows_of(b * per_home + c)],
            send_sem=back_send.at[c, d], recv_sem=back_recv.at[c, b],
            device_id=(s, owner), device_id_type=MESH)

    def own_back(c):
        at = rows_of(b * per_home + c)
        return pltpu.make_async_copy(f1.at[at], out.at[at], own_sem.at[c])

    def rotate(d, send):
        i = band_at(d)
        poly = polynomial(i)

        def rotate_rows(c, carry):
            left = tuple(
                jnp.concatenate([ref[rows_of(k * per_home + c)] for k in range(n_b)], axis=1)
                for ref in (xh, xl))
            f1[rows_of(i * per_home + c)] = dot3(left, poly) * gain
            send(c, d).start()
            return carry

        lax.fori_loop(0, per_home, rotate_rows, 0)

    for d in far_first:
        rotate(d, back)
    rotate(0, lambda c, d: own_back(c))

    def finish(c, carry):
        for d in range(1, n_b):
            to_home(c, d).wait_send()
            back(c, d).wait_send()
            source = band_at(d)
            pltpu.make_async_remote_copy(
                src_ref=f1.at[rows_of(c)],
                dst_ref=out.at[rows_of(source * per_home + c)],
                send_sem=back_send.at[c, d], recv_sem=back_recv.at[c, source],
                device_id=(s, source), device_id_type=MESH).wait_recv()
        own_back(c).wait()
        return carry

    lax.fori_loop(0, per_home, finish, 0)


def per_device(n_s, n_b, vectors, blocks, neighbours):
    elem, count, basis, _ = blocks.shape
    panel = vectors.shape[1]
    total = elem * n_s
    ids = lax.axis_index("space") * elem + jnp.arange(elem, dtype=jnp.int32)
    slots = (neighbours - ids[:, None] + REACH + total) % total
    weights = jax.nn.one_hot(slots, SPAN, dtype=F32).reshape(-1)

    rows = elem * basis
    per_home = elem // n_b
    devices = n_s * n_b
    block_rows = panel // LANES * panel
    need = n_b * (n_b - 1) // 2 * block_rows
    parts = 2 if need % (16 * devices) == 0 else 1
    unit = 8 * devices * parts
    packed = -(-need // unit) * unit
    steps = n_s.bit_length() - 1
    padded = (elem + 2 * REACH) * basis
    dma = pltpu.SemaphoreType.DMA
    any_spec = pl.BlockSpec(memory_space=pl.ANY)
    flops = 2 * rows * panel * 3 * (2 * SPAN * basis) + 6 * rows * panel * 1024 * 3
    return pl.pallas_call(
        functools.partial(main_kernel, n_s, n_b, elem, basis, panel, parts),
        out_shape=jax.ShapeDtypeStruct((rows, panel), F32),
        in_specs=[pl.BlockSpec(memory_space=pltpu.SMEM), any_spec, any_spec],
        out_specs=any_spec,
        scratch_shapes=[
            pltpu.VMEM((rows, panel), F32),
            pltpu.VMEM((padded, panel), BF16),
            pltpu.VMEM((padded, panel), BF16),
            pltpu.VMEM((padded, panel), BF16),
            pltpu.VMEM((padded, panel), BF16),
            pltpu.VMEM((elem, basis, SPAN * basis), BF16),
            pltpu.VMEM((elem, basis, SPAN * basis), BF16),
            pltpu.VMEM((rows, panel), F32),
            pltpu.VMEM((rows, panel), F32),
            pltpu.VMEM((packed, LANES), F32),
            pltpu.VMEM((parts, packed // parts, LANES), F32),
            pltpu.VMEM((packed, LANES), F32),
            pltpu.VMEM((2, 2, REACH * basis, panel), F32),
            pltpu.VMEM((3, count, basis, basis), F32),
            pltpu.VMEM((block_rows, LANES), F32),
            pltpu.VMEM((block_rows, LANES), F32),
            pltpu.VMEM((n_b, block_rows, LANES), F32),
            dma, dma((3,)), dma((2, 2)), dma((2, 2)),
            dma((per_home, n_b)), dma((per_home, n_b)),
            dma((2, steps, parts)), dma((2, steps, parts)),
            dma((2, n_b, parts)), dma((2, n_b, parts)),
            dma((2, steps)), dma((2, steps)), dma((n_b,)), dma((n_b,)),
            dma((per_home, n_b)), dma((per_home, n_b)), dma((per_home,)),
        ],
        compiler_params=pltpu.CompilerParams(
            collective_id=0, has_side_effects=True, vmem_limit_bytes=60 * 2**20),
        cost_estimate=pl.CostEstimate(
            flops=flops, bytes_accessed=40 * 2**20, transcendentals=0),
        name="filter_and_rotate",
    )(weights, vectors, blocks)


def solution(mesh):
    return jax.shard_map(
        functools.partial(per_device, mesh.shape["space"], mesh.shape["band"]),
        mesh=mesh,
        in_specs=(P("space", "band"), P("space", None, None, None), P("space", None)),
        out_specs=P("space", "band"),
        check_vma=False,
    )
```
